256 devices in a mesh: span: 8 (over x_lo, y), wide: 32 (over x_hi, z, core).
Axes of the slice: x: 4 (x_hi: 2, x_lo: 2; x = x_hi * 2 + x_lo), y: 4, z: 8, core: 2. Of those that a mesh axis runs over, the one named last changes fastest.
Arguments:
- queries: bfloat16 [36864, 4096], P(('span', 'wide')), may hold values from -28 to 28
- keys: bfloat16 [36864, 4096], P(('span', 'wide')), may hold values from -9.6 to 9.6
- values: bfloat16 [36864, 4096], P(('span', 'wide')), may hold values from -12 to 12
- windows: int32 [96, 12], replicated, may hold values from -1 to 95, as said below
Outputs:
- attended: bfloat16 [36864, 4096], P(('span', 'wide'))
The draws below stay inside these ranges and needn't reach their ends.
Inputs may be any that keep to these rules, and one draw needn't show every extreme that they name: `windows`: row i lists the tiles that tile i attends to, where a tile's time tile is its index // 6: every listed tile lies at most one time tile from tile i's, the entries of a row are distinct, tile i is in row i, and -1 marks an empty slot.
All inputs are finite; a program needn't handle non-finite values.
Results may differ from the reference program's by a relative error of at most 0.0031.
Values may be sent and summed in bfloat16 or wider, within the bound.
A program may use at most 128 MiB of HBM per device.

```python
import jax
import jax.numpy as jnp
from jax import lax

HD = 128
HEADS = 32
TILE = 384
HT = 2
WT = 3
TT = 16
TILES = 96
TOKENS = 36864


KEY_SPREAD = 1.6


def draw_keys(key, part):
    key = jax.random.fold_in(key, 2)
    own = jax.random.normal(key, (TOKENS, HEADS * HD), jnp.float32) * KEY_SPREAD
    result = jnp.clip(own, -6.0 * KEY_SPREAD, 6.0 * KEY_SPREAD)
    return result.astype(jnp.bfloat16)


def draw_queries(key, part):
    key = jax.random.fold_in(key, 1)
    own = jax.random.normal(key, (TOKENS, HEADS * HD), jnp.float32) * KEY_SPREAD
    result = jnp.clip(own, -6.0 * KEY_SPREAD, 6.0 * KEY_SPREAD)
    return result.astype(jnp.bfloat16)


def draw_windows(key, part):
    key = jax.random.fold_in(key, 7)
    plane = HT * WT
    tile_ids = jnp.arange(TILES, dtype=jnp.int32)
    time_tile = tile_ids // plane
    row_tile = tile_ids // WT % HT
    column_tile = tile_ids % WT
    picks = jax.random.randint(key, (TILES, 3, 2), 0, 2).astype(jnp.int32)
    columns = []
    for offset in (-1, 0, 1):
        moved = time_tile + offset
        inside = (moved >= 0) & (moved < TT)
        row_start = jnp.clip(row_tile - picks[:, offset + 1, 0], 0, HT - 2)
        column_start = jnp.clip(column_tile - picks[:, offset + 1, 1], 0, WT - 2)
        for down in (0, 1):
            for across in (0, 1):
                entry = moved * plane + (row_start + down) * WT + (column_start + across)
                columns.append(jnp.where(inside, entry, -1))
    return jnp.stack(columns, axis=1).astype(jnp.int32)


def level_of(stream_key, dims, cuts, least, largest):
    def one(position, shards_of):
        steps = jax.random.uniform(jax.random.fold_in(jax.random.fold_in(stream_key, 6), position), (shards_of,), jnp.float32, least / len(cuts), largest / len(cuts))
        return jnp.repeat(jnp.exp(steps), dims[position] // shards_of).reshape((-1,) + (1,) * (len(dims) - position - 1))

    factor_of = one(*cuts[0])
    for cut in cuts[1:]:
        factor_of = factor_of * one(*cut)
    return factor_of


def bell_draw(rng, extent, deviation, most, shards=(), kind=jnp.bfloat16):
    values = deviation * jax.random.normal(rng, extent, jnp.float32)
    if shards:
        values = values * level_of(rng, extent, shards, -0.22, 0.18)
    return jnp.clip(values, -most, most).astype(kind)


def setup_inputs(seed: int = 0) -> dict:
    streams_of = jax.random.split(jax.random.key(seed), 5)
    queries = draw_queries(jax.random.fold_in(streams_of[4], 71), 0)
    keys = draw_keys(jax.random.fold_in(streams_of[4], 71), 0)
    values = bell_draw(streams_of[2], (TOKENS, HEADS * HD), 2.0, 12.0, ((0, 256),))
    windows = draw_windows(jax.random.fold_in(streams_of[4], 71), 0)
    return {"queries": queries, "keys": keys, "values": values, "windows": windows}


NEG_FILL = -1.0e30


def reference(queries, keys, values, windows):
    score_scale = HD ** -0.5
    query_tiles = queries.reshape(TILES, TILE, HEADS, HD)
    key_tiles = keys.reshape(TILES, TILE, HEADS, HD)
    value_tiles = values.reshape(TILES, TILE, HEADS, HD)

    def one_tile(index):
        window_row = windows[index]
        allowed = window_row >= 0
        listed = jnp.where(allowed, window_row, 0).astype(jnp.int32)
        picked_keys = key_tiles[listed].astype(jnp.float32)
        picked_values = value_tiles[listed].astype(jnp.float32)
        query_block = query_tiles[index].astype(jnp.float32)
        scores = jnp.einsum("qhd,nthd->hqnt", query_block, picked_keys) * score_scale
        masked = jnp.where(allowed[None, None, :, None], scores, NEG_FILL)
        highest = jnp.max(masked, axis=(2, 3), keepdims=True)
        expo = jnp.exp(masked - highest)
        summed = jnp.sum(expo, axis=(2, 3))
        weights = lax.optimization_barrier(expo.astype(jnp.bfloat16)).astype(jnp.float32)
        mixed = jnp.einsum("hqnt,nthd->qhd", weights, picked_values)
        return (mixed / jnp.transpose(summed)[:, :, None]).astype(jnp.bfloat16)

    result = lax.map(one_tile, jnp.arange(TILES, dtype=jnp.int32))
    return result.reshape(TOKENS, HEADS * HD)
```

```python
import functools
import math

import jax
import jax.numpy as jnp
from jax import lax
from jax.experimental import pallas as pl
from jax.experimental.pallas import tpu as pltpu
from jax.sharding import PartitionSpec as P

HD = 128
TILE = 384
PLANE = 6
NBR = 12
GANG = 8
UNIT = 48
PACK = 4
MESH = pl.DeviceIdType.MESH
SCALE = HD**-0.5 * math.log2(math.e)


def kernel(
    spans, wides,
    key_at, value_at, there, queries, keys, values, out,
    kbuf, vbuf, qbuf, obuf, scores,
    own_sem, ksem, vsem, qsem, send_sem, halo_sem, fwd_sem, osend_sem, orecv_sem,
):
    me = lax.axis_index("wide")
    span = lax.axis_index("span")
    above = lax.rem(span + 1, spans)
    below = lax.rem(span + spans - 1, spans)
    part = queries.shape[0]
    units = TILE // UNIT
    own_units = wides * part
    own_tiles = own_units // units
    halo = PLANE * units
    upper = halo + own_units
    half = wides // 2
    gangs = wides // GANG
    gang = me // GANG
    place = lax.rem(me, GANG)

    def columns(ref, head):
        return ref.at[:, :, pl.ds(pl.multiple_of(head * HD, HD), HD)]

    def block(ref, first, index):
        return ref.at[pl.ds(first + index * part, part)]

    def target(i):
        to = lax.rem(gang - i // GANG + gangs, gangs)
        return to * GANG + lax.rem(place + lax.rem(i, GANG), GANG)

    def source(i):
        at = lax.rem(gang + i // GANG, gangs)
        return at * GANG + lax.rem(place - lax.rem(i, GANG) + GANG, GANG)

    own = [
        pltpu.make_async_copy(columns(keys, me), block(kbuf, halo, me), own_sem.at[0]),
        pltpu.make_async_copy(columns(values, me), block(vbuf, halo, me), own_sem.at[1]),
        pltpu.make_async_copy(columns(queries, me), block(qbuf, 0, me), own_sem.at[2]),
    ]
    for copy in own:
        copy.start()

    barrier = pltpu.get_barrier_semaphore()

    def greet(i, carry):
        pl.semaphore_signal(barrier, inc=1, device_id=(span, target(i)), device_id_type=MESH)
        return carry

    lax.fori_loop(1, wides, greet, 0)
    for neighbour in (above, below):
        pl.semaphore_signal(barrier, inc=1, device_id=(neighbour, me), device_id_type=MESH)
    pl.semaphore_wait(barrier, wides + 1)

    def send(kind, i):
        ref, buf, first, sem = (
            (keys, kbuf, halo, ksem),
            (values, vbuf, halo, vsem),
            (queries, qbuf, 0, qsem),
        )[kind]
        to = target(i)
        pltpu.make_async_remote_copy(
            src_ref=columns(ref, to),
            dst_ref=block(buf, first, me),
            send_sem=send_sem.at[kind],
            recv_sem=sem.at[me],
            device_id=(span, to),
            device_id_type=MESH,
        ).start()

    def send_step(kind):
        def step(i, carry):
            send(kind, i)
            return carry
        return step

    def arrived(buf, first, sem, u):
        piece = block(buf, first, u)
        pltpu.make_async_copy(piece, piece, sem.at[u]).wait()

    def forward(kind, buf, u):
        late = u // half
        piece = block(buf, halo, u)
        place_there = block(buf, (1 - late) * upper, lax.rem(u, half))
        pltpu.make_async_remote_copy(
            src_ref=piece,
            dst_ref=place_there,
            send_sem=fwd_sem.at[kind],
            recv_sem=halo_sem.at[2 * kind + 1 - late],
            device_id=(late * above + (1 - late) * below, me),
            device_id_type=MESH,
        ).start()

    lax.fori_loop(1, wides, send_step(0), 0)
    lax.fori_loop(1, wides, send_step(1), 0)
    vbuf[pl.ds(upper + halo, units)] = jnp.zeros((units, UNIT, HD), jnp.bfloat16)

    own[0].wait()
    forward(0, kbuf, me)

    def pass_keys(i, carry):
        u = source(i)
        arrived(kbuf, halo, ksem, u)
        forward(0, kbuf, u)
        return carry

    lax.fori_loop(1, wides, pass_keys, 0)
    own[1].wait()
    forward(1, vbuf, me)

    def pass_values(i, carry):
        u = source(i)
        arrived(vbuf, halo, vsem, u)
        forward(1, vbuf, u)
        send(2, i)
        return carry

    lax.fori_loop(1, wides, pass_values, 0)
    own[2].wait()

    for kind, buf in ((0, kbuf), (1, vbuf)):
        for side, first in ((0, 0), (1, upper)):
            region = buf.at[pl.ds(first, halo)]
            pltpu.make_async_copy(region, region, halo_sem.at[2 * kind + side]).wait()

    def gang_at(step):
        return lax.rem(gang + step // 3, gangs)

    def tile_at(step):
        return gang_at(step) * 3 + lax.rem(step, 3)

    def await_queries(step):
        @pl.when(lax.rem(step, 3) == 0)
        def _():
            def one(j, carry):
                u = gang_at(step) * GANG + j

                @pl.when(u != me)
                def _():
                    arrived(qbuf, 0, qsem, u)

                return carry

            lax.fori_loop(0, GANG, one, 0)

    first_tile = span * own_tiles

    def whole(ref, first):
        return jnp.concatenate([ref[first + j] for j in range(units)], axis=0)

    def key_tile(tile, slot):
        return whole(kbuf, key_at[first_tile + tile, slot])

    def value_tile(tile, slot):
        value = whole(vbuf, value_at[first_tile + tile, slot])
        ones = jnp.full((TILE, HD), there[first_tile + tile, slot]).astype(jnp.bfloat16)
        return jnp.concatenate([value, ones], axis=1)

    def load_queries(tile):
        return qbuf[pl.ds(tile * units, units)].reshape(TILE, HD)

    def score(tile, query, pack, highest):
        key = jnp.concatenate([key_tile(tile, pack * PACK + j) for j in range(PACK)], axis=0)
        fresh = lax.dot_general(
            query, key, (((1,), (1,)), ((), ())), preferred_element_type=jnp.float32
        )
        scores[pack] = fresh
        for at in range(0, PACK * TILE, HD):
            highest = jnp.maximum(highest, fresh[:, at : at + HD])
        return highest

    def mix(tile, shift, pack, total):
        value = jnp.concatenate([value_tile(tile, pack * PACK + j) for j in range(PACK)], axis=0)
        weights = jnp.exp2(scores[pack] * SCALE - shift).astype(jnp.bfloat16)
        part = jnp.dot(weights, value, preferred_element_type=jnp.float32)
        return part if total is None else total + part

    def lowest():
        return jnp.full((TILE, HD), -jnp.inf, jnp.float32)

    def shift_of(highest):
        return jnp.max(highest, axis=1, keepdims=True) * SCALE

    def finish(step, total):
        tile = tile_at(step)
        mixed = (total[:, :HD] / total[:, HD:]).astype(jnp.bfloat16)
        obuf[pl.ds(tile * units, units)] = mixed.reshape(units, UNIT, HD)
        begin = 3 * lax.rem(step, 3) - 1

        def one(j, carry):
            @pl.when(begin + j >= 0)
            def _():
                u = gang_at(step) * GANG + begin + j

                @pl.when(u == me)
                def _():
                    pltpu.make_async_copy(
                        block(obuf, 0, u), columns(out, me), orecv_sem
                    ).start()

                @pl.when(u != me)
                def _():
                    pltpu.make_async_remote_copy(
                        src_ref=block(obuf, 0, u),
                        dst_ref=columns(out, me),
                        send_sem=osend_sem,
                        recv_sem=orecv_sem,
                        device_id=(span, u),
                        device_id_type=MESH,
                    ).start()

            return carry

        lax.fori_loop(0, 3, one, 0)

    packs = NBR // PACK
    await_queries(0)
    query = load_queries(tile_at(0))
    highest = lowest()
    for pack in range(packs):
        highest = score(tile_at(0), query, pack, highest)

    def turn(step, shift):
        await_queries(step + 1)
        tile, later = tile_at(step), tile_at(step + 1)
        query = load_queries(later)
        highest, total = lowest(), None
        for pack in range(packs):
            total = mix(tile, shift, pack, total)
            highest = score(later, query, pack, highest)
        finish(step, total)
        return shift_of(highest)

    shift = lax.fori_loop(0, own_tiles - 1, turn, shift_of(highest))
    total = None
    for pack in range(packs):
        total = mix(tile_at(own_tiles - 1), shift, pack, total)
    finish(own_tiles - 1, total)

    sent = (wides - 1) * HD
    for kind, ref in enumerate((keys, values, queries)):
        region = ref.at[:, :, pl.ds(0, sent)]
        pltpu.make_async_copy(region, region, send_sem.at[kind]).wait()
    for kind, buf in ((0, kbuf), (1, vbuf)):
        region = buf.at[pl.ds(halo, own_units)]
        pltpu.make_async_copy(region, region, fwd_sem.at[kind]).wait()
    region = obuf.at[pl.ds(0, (wides - 1) * part)]
    pltpu.make_async_copy(region, region, osend_sem).wait()
    pltpu.make_async_copy(out, out, orecv_sem).wait()


def body(spans, wides, queries, keys, values, windows):
    rows, width = queries.shape
    part = rows // UNIT
    units = TILE // UNIT
    own_units = wides * part
    near = own_units + 2 * PLANE * units
    own_tiles = own_units // units
    tiles = jnp.arange(windows.shape[0], dtype=jnp.int32)[:, None]
    first = tiles // own_tiles * own_tiles
    listed = windows >= 0
    key_at = (jnp.where(listed, windows, tiles) - first + PLANE) * units
    value_at = jnp.where(listed, key_at, near)
    cut = [a.reshape(part, UNIT, width) for a in (queries, keys, values)]
    dma = pltpu.SemaphoreType.DMA
    out = pl.pallas_call(
        functools.partial(kernel, spans, wides),
        out_shape=jax.ShapeDtypeStruct((part, UNIT, width), jnp.bfloat16),
        in_specs=[pl.BlockSpec(memory_space=pltpu.SMEM)] * 3
        + [pl.BlockSpec(memory_space=pl.ANY)] * 3,
        out_specs=pl.BlockSpec(memory_space=pl.ANY),
        scratch_shapes=[
            pltpu.VMEM((near, UNIT, HD), jnp.bfloat16),
            pltpu.VMEM((near + units, UNIT, HD), jnp.bfloat16),
            pltpu.VMEM((own_units, UNIT, HD), jnp.bfloat16),
            pltpu.VMEM((own_units, UNIT, HD), jnp.bfloat16),
            pltpu.VMEM((NBR // PACK, TILE, PACK * TILE), jnp.float32),
            dma((3,)),
            dma((wides,)),
            dma((wides,)),
            dma((wides,)),
            dma((3,)),
            dma((4,)),
            dma((2,)),
            dma(()),
            dma(()),
        ],
        compiler_params=pltpu.CompilerParams(
            collective_id=0, has_side_effects=True, vmem_limit_bytes=40 << 20
        ),
        name="attend",
    )(key_at, value_at, listed.astype(jnp.float32), *cut)
    return out.reshape(rows, width)


def solution(mesh):
    return jax.shard_map(
        functools.partial(body, mesh.shape["span"], mesh.shape["wide"]),
        mesh=mesh,
        in_specs=(
            P(("span", "wide"), None),
            P(("span", "wide"), None),
            P(("span", "wide"), None),
            P(),
        ),
        out_specs=P(("span", "wide"), None),
        check_vma=False,
    )
```

```python
import functools
import math

import jax
import jax.numpy as jnp
from jax import lax
from jax.experimental import pallas as pl
from jax.experimental.pallas import tpu as pltpu
from jax.sharding import PartitionSpec as P

HD = 128
TILE = 384
PLANE = 6
NBR = 12
GANG = 8
UNIT = 48
PACK = 4
SPLITS = {2: ((0, 2, 0), (2, 1, 1)), 5: ((0, 1, 0), (1, 2, 1)), -1: ((0, 3, 0),)}
GIVES = (
    ((0, 0, 0, 3), (1, 0, 3, 3), (2, 0, 6, 2)),
    ((2, 2, 8, 1), (3, 0, 9, 3), (4, 0, 12, 3), (5, 0, 15, 1)),
    ((5, 1, 16, 2), (6, 0, 18, 3), (7, 0, 21, 3)),
)
MESH = pl.DeviceIdType.MESH
SCALE = HD**-0.5 * math.log2(math.e)


def kernel(
    spans, wides,
    windows, queries, keys, values, out,
    kbuf, vbuf, qbuf, obuf, scores,
    own_sem, ksem, vsem, qsem, send_sem, halo_sem, fwd_sem, osend_sem, orecv_sem,
):
    me = lax.axis_index("wide")
    span = lax.axis_index("span")
    above = lax.rem(span + 1, spans)
    below = lax.rem(span + spans - 1, spans)
    part = queries.shape[0]
    units = TILE // UNIT
    own_units = wides * part
    own_tiles = own_units // units
    halo = PLANE * units
    upper = halo + own_units
    half = wides // 2
    deep = half // 2
    side, depth, core = lax.div(me, half), lax.rem(lax.div(me, 2), deep), lax.rem(me, 2)

    def columns(ref, head):
        return ref.at[:, :, pl.ds(pl.multiple_of(head * HD, HD), HD)]

    def block(ref, first, index):
        return ref.at[pl.ds(first + index * part, part)]

    def peers(k, outward):
        up, down = depth + k, depth - k
        up = jnp.where(up >= deep, up - deep, up)
        down = jnp.where(down < 0, down + deep, down)
        found = []
        for j in range(4):
            there = core if j % 2 == 0 else 1 - core
            far = jnp.where(there == 1, up, down) if outward else jnp.where(core == 1, down, up)
            found.append((side if j < 2 else 1 - side, far * 2 + there))
        return found

    def every(step, outward):
        for peer in peers(0, outward)[1:]:
            step(*peer)

        def ring(k, carry):
            for peer in peers(k, outward):
                step(*peer)
            return carry

        lax.fori_loop(1, deep, ring, 0)

    own = [
        pltpu.make_async_copy(columns(keys, me), block(kbuf, halo, me), own_sem.at[0]),
        pltpu.make_async_copy(columns(values, me), block(vbuf, halo, me), own_sem.at[1]),
    ]
    for copy in own:
        copy.start()
    place_in_gang = lax.rem(me, GANG)
    own_tile = lax.div(me * part, units)
    whole_block = (place_in_gang != 2) & (place_in_gang != 5)
    for p in range(part):
        unit = me * part + p
        pltpu.make_async_copy(
            columns(queries, me).at[p], qbuf.at[unit], qsem.at[lax.div(unit, units)]
        ).start()

    barrier = pltpu.get_barrier_semaphore()

    def greet(row, place):
        to = row * half + place
        pl.semaphore_signal(barrier, inc=1, device_id=(span, to), device_id_type=MESH)

    every(greet, True)
    for neighbour in (above, below):
        pl.semaphore_signal(barrier, inc=1, device_id=(neighbour, me), device_id_type=MESH)
    pl.semaphore_wait(barrier, wides + 1)

    def send(kind, row, place):
        ref, buf, sem = ((keys, kbuf, ksem), (values, vbuf, vsem))[kind]
        to = row * half + place
        pltpu.make_async_remote_copy(
            src_ref=columns(ref, to),
            dst_ref=block(buf, halo, me),
            send_sem=send_sem.at[kind],
            recv_sem=sem.at[me],
            device_id=(span, to),
            device_id_type=MESH,
        ).start()

    def send_queries(row, place):
        to = row * half + place
        for member, pieces in SPLITS.items():
            mine = member == place_in_gang if member >= 0 else whole_block

            @pl.when(mine)
            def _():
                for begin, count, ahead in pieces:
                    pltpu.make_async_remote_copy(
                        src_ref=columns(queries, to).at[pl.ds(begin, count)],
                        dst_ref=qbuf.at[pl.ds(me * part + begin, count)],
                        send_sem=send_sem.at[2],
                        recv_sem=qsem.at[own_tile + ahead],
                        device_id=(span, to),
                        device_id_type=MESH,
                    ).start()

    def arrived(buf, sem, u):
        piece = block(buf, halo, u)
        pltpu.make_async_copy(piece, piece, sem.at[u]).wait()

    def forward(kind, buf, row, place):
        pltpu.make_async_remote_copy(
            src_ref=block(buf, halo, row * half + place),
            dst_ref=block(buf, (1 - row) * upper, place),
            send_sem=fwd_sem.at[kind],
            recv_sem=halo_sem.at[2 * kind + 1 - row],
            device_id=(row * above + (1 - row) * below, me),
            device_id_type=MESH,
        ).start()

    every(functools.partial(send, 0), True)
    every(functools.partial(send, 1), True)
    vbuf[pl.ds(upper + halo, units)] = jnp.zeros((units, UNIT, HD), jnp.bfloat16)

    def pass_on(kind, buf, sem):
        def step(row, place):
            arrived(buf, sem, row * half + place)
            forward(kind, buf, row, place)

        own[kind].wait()
        forward(kind, buf, side, depth * 2 + core)
        every(step, False)

    pass_on(0, kbuf, ksem)
    every(send_queries, True)
    pass_on(1, vbuf, vsem)

    for kind, buf in ((0, kbuf), (1, vbuf)):
        for end, first in ((0, 0), (1, upper)):
            region = buf.at[pl.ds(first, halo)]
            pltpu.make_async_copy(region, region, halo_sem.at[2 * kind + end]).wait()

    def tile_at(step):
        begin = lax.div(depth * 3 + 3, 4) - core
        turned = begin + (1 - 2 * core) * lax.div(step, 2)
        return lax.rem(side + step, 2) * PLANE + lax.rem(turned + PLANE, PLANE)

    def await_queries(step):
        tile = qbuf.at[pl.ds(tile_at(step) * units, units)]
        pltpu.make_async_copy(tile, tile, qsem.at[tile_at(step)]).wait()

    first_tile = span * own_tiles

    def whole(ref, first):
        return jnp.concatenate([ref[first + j] for j in range(units)], axis=0)

    def listed(tile, slot):
        entry = windows[slot, first_tile + tile]
        there = jnp.minimum(entry, 0) + 1
        near = jnp.clip(entry - first_tile + PLANE, 0, own_tiles + 2 * PLANE - 1)
        return there, there * near

    def key_tile(tile, slot):
        there, index = listed(tile, slot)
        return whole(kbuf, (index + (1 - there) * (tile + PLANE)) * units)

    def value_tile(tile, slot):
        there, index = listed(tile, slot)
        value = whole(vbuf, (index + (1 - there) * (own_tiles + 2 * PLANE)) * units)
        ones = jnp.full((TILE, HD), there.astype(jnp.float32)).astype(jnp.bfloat16)
        return jnp.concatenate([value, ones], axis=1)

    def load_queries(tile):
        return qbuf[pl.ds(tile * units, units)].reshape(TILE, HD)

    def score(tile, query, pack, highest):
        key = jnp.concatenate([key_tile(tile, pack * PACK + j) for j in range(PACK)], axis=0)
        fresh = lax.dot_general(
            query, key, (((1,), (1,)), ((), ())), preferred_element_type=jnp.float32
        )
        scores[pack] = fresh
        for at in range(0, PACK * TILE, HD):
            highest = jnp.maximum(highest, fresh[:, at : at + HD])
        return highest

    def mix(tile, shift, pack, total):
        value = jnp.concatenate([value_tile(tile, pack * PACK + j) for j in range(PACK)], axis=0)
        weights = jnp.exp2(scores[pack] * SCALE - shift).astype(jnp.bfloat16)
        part = jnp.dot(weights, value, preferred_element_type=jnp.float32)
        return part if total is None else total + part

    def lowest():
        return jnp.full((TILE, HD), -jnp.inf, jnp.float32)

    def shift_of(highest):
        return jnp.max(highest, axis=1, keepdims=True) * SCALE

    def finish(step, total):
        tile = tile_at(step)
        mixed = (total[:, :HD] / total[:, HD:]).astype(jnp.bfloat16)
        obuf[pl.ds(tile * units, units)] = mixed.reshape(units, UNIT, HD)

        gang = lax.div(tile, 3) * GANG
        for turn_of, pieces in enumerate(GIVES):
            @pl.when(lax.rem(tile, 3) == turn_of)
            def _():
                for place, begin, unit, count in pieces:
                    give(gang + place, begin, gang * part + unit, count)

    def give(u, begin, unit, count):
        mixed = obuf.at[pl.ds(unit, count)]
        home = columns(out, me).at[pl.ds(begin, count)]

        @pl.when(u == me)
        def _():
            pltpu.make_async_copy(mixed, home, orecv_sem).start()

        @pl.when(u != me)
        def _():
            pltpu.make_async_remote_copy(
                src_ref=mixed,
                dst_ref=home,
                send_sem=osend_sem,
                recv_sem=orecv_sem,
                device_id=(span, u),
                device_id_type=MESH,
            ).start()

    packs = NBR // PACK
    await_queries(0)
    query = load_queries(tile_at(0))
    highest = lowest()
    for pack in range(packs):
        highest = score(tile_at(0), query, pack, highest)

    def turn(step, shift):
        await_queries(step + 1)
        tile, later = tile_at(step), tile_at(step + 1)
        query = load_queries(later)
        highest, total = lowest(), None
        for pack in range(packs):
            total = mix(tile, shift, pack, total)
            highest = score(later, query, pack, highest)
        finish(step, total)
        return shift_of(highest)

    shift = lax.fori_loop(0, own_tiles - 1, turn, shift_of(highest))
    total = None
    for pack in range(packs):
        total = mix(tile_at(own_tiles - 1), shift, pack, total)
    finish(own_tiles - 1, total)

    sent = (wides - 1) * HD
    for kind, ref in enumerate((keys, values, queries)):
        region = ref.at[:, :, pl.ds(0, sent)]
        pltpu.make_async_copy(region, region, send_sem.at[kind]).wait()
    for kind, buf in ((0, kbuf), (1, vbuf)):
        region = buf.at[pl.ds(halo, own_units)]
        pltpu.make_async_copy(region, region, fwd_sem.at[kind]).wait()
    region = obuf.at[pl.ds(0, (wides - 1) * part)]
    pltpu.make_async_copy(region, region, osend_sem).wait()
    pltpu.make_async_copy(out, out, orecv_sem).wait()


def body(spans, wides, queries, keys, values, windows):
    rows, width = queries.shape
    part = rows // UNIT
    units = TILE // UNIT
    own_units = wides * part
    near = own_units + 2 * PLANE * units
    cut = [a.reshape(part, UNIT, width) for a in (queries, keys, values)]
    dma = pltpu.SemaphoreType.DMA
    out = pl.pallas_call(
        functools.partial(kernel, spans, wides),
        out_shape=jax.ShapeDtypeStruct((part, UNIT, width), jnp.bfloat16),
        in_specs=[pl.BlockSpec(memory_space=pltpu.SMEM)]
        + [pl.BlockSpec(memory_space=pltpu.HBM)] * 3,
        out_specs=pl.BlockSpec(memory_space=pl.ANY),
        scratch_shapes=[
            pltpu.VMEM((near, UNIT, HD), jnp.bfloat16),
            pltpu.VMEM((near + units, UNIT, HD), jnp.bfloat16),
            pltpu.VMEM((own_units, UNIT, HD), jnp.bfloat16),
            pltpu.VMEM((own_units, UNIT, HD), jnp.bfloat16),
            pltpu.VMEM((NBR // PACK, TILE, PACK * TILE), jnp.float32),
            dma((2,)),
            dma((wides,)),
            dma((wides,)),
            dma((own_units // units,)),
            dma((3,)),
            dma((4,)),
            dma((2,)),
            dma(()),
            dma(()),
        ],
        compiler_params=pltpu.CompilerParams(
            collective_id=0, has_side_effects=True, vmem_limit_bytes=60 << 20
        ),
        name="attend",
    )(windows.T, *cut)
    return out.reshape(rows, width)


def solution(mesh):
    return jax.shard_map(
        functools.partial(body, mesh.shape["span"], mesh.shape["wide"]),
        mesh=mesh,
        in_specs=(
            P(("span", "wide"), None),
            P(("span", "wide"), None),
            P(("span", "wide"), None),
            P(),
        ),
        out_specs=P(("span", "wide"), None),
        check_vma=False,
    )
```

```python
import functools
import math

import jax
import jax.numpy as jnp
from jax import lax
from jax.experimental import pallas as pl
from jax.experimental.pallas import tpu as pltpu
from jax.sharding import PartitionSpec as P

HD = 128
TILE = 384
PLANE = 6
NBR = 12
GANG = 8
UNIT = 48
PACK = 4
SPLITS = {2: ((0, 2, 0), (2, 1, 1)), 5: ((0, 1, 0), (1, 2, 1)), -1: ((0, 3, 0),)}
GIVES = (
    ((0, 0, 0, 3), (1, 0, 3, 3), (2, 0, 6, 2)),
    ((2, 2, 8, 1), (3, 0, 9, 3), (4, 0, 12, 3), (5, 0, 15, 1)),
    ((5, 1, 16, 2), (6, 0, 18, 3), (7, 0, 21, 3)),
)
MESH = pl.DeviceIdType.MESH
SCALE = HD**-0.5 * math.log2(math.e)


def kernel(
    spans, wides,
    windows, queries, keys, values, out,
    kbuf, vbuf, qbuf, obuf, scores,
    own_sem, ksem, vsem, qsem, send_sem, halo_sem, fwd_sem, osend_sem, orecv_sem,
):
    me = lax.axis_index("wide")
    span = lax.axis_index("span")
    above = lax.rem(span + 1, spans)
    below = lax.rem(span + spans - 1, spans)
    part = queries.shape[0]
    units = TILE // UNIT
    own_units = wides * part
    own_tiles = own_units // units
    halo = PLANE * units
    upper = halo + own_units
    half = wides // 2
    deep = half // 2
    side, depth, core = lax.div(me, half), lax.rem(lax.div(me, 2), deep), lax.rem(me, 2)

    def columns(ref, head):
        return ref.at[:, :, pl.ds(pl.multiple_of(head * HD, HD), HD)]

    def block(ref, first, index):
        return ref.at[pl.ds(first + index * part, part)]

    def peers(k, outward):
        up, down = depth + k, depth - k
        up = jnp.where(up >= deep, up - deep, up)
        down = jnp.where(down < 0, down + deep, down)
        found = []
        for j in range(4):
            there = core if j % 2 == 0 else 1 - core
            far = jnp.where(there == 1, up, down) if outward else jnp.where(core == 1, down, up)
            found.append((side if j < 2 else 1 - side, far * 2 + there))
        return found

    def every(step, outward):
        for peer in peers(0, outward)[1:]:
            step(*peer)

        def ring(k, carry):
            for peer in peers(k, outward):
                step(*peer)
            return carry

        lax.fori_loop(1, deep, ring, 0)

    own = [
        pltpu.make_async_copy(columns(keys, me), block(kbuf, halo, me), own_sem.at[0]),
        pltpu.make_async_copy(columns(values, me), block(vbuf, halo, me), own_sem.at[1]),
    ]
    for copy in own:
        copy.start()
    place_in_gang = lax.rem(me, GANG)
    own_tile = lax.div(me * part, units)
    whole_block = (place_in_gang != 2) & (place_in_gang != 5)
    for p in range(part):
        unit = me * part + p
        pltpu.make_async_copy(
            columns(queries, me).at[p], qbuf.at[unit], qsem.at[lax.div(unit, units)]
        ).start()

    barrier = pltpu.get_barrier_semaphore()

    def greet(row, place):
        to = row * half + place
        pl.semaphore_signal(barrier, inc=1, device_id=(span, to), device_id_type=MESH)

    every(greet, True)
    for neighbour in (above, below):
        pl.semaphore_signal(barrier, inc=1, device_id=(neighbour, me), device_id_type=MESH)
    pl.semaphore_wait(barrier, wides + 1)

    def send(kind, row, place):
        ref, buf, sem = ((keys, kbuf, ksem), (values, vbuf, vsem))[kind]
        to = row * half + place
        pltpu.make_async_remote_copy(
            src_ref=columns(ref, to),
            dst_ref=block(buf, halo, me),
            send_sem=send_sem.at[kind],
            recv_sem=sem.at[me],
            device_id=(span, to),
            device_id_type=MESH,
        ).start()

    def send_queries(row, place):
        to = row * half + place
        for member, pieces in SPLITS.items():
            mine = member == place_in_gang if member >= 0 else whole_block

            @pl.when(mine)
            def _():
                for begin, count, ahead in pieces:
                    pltpu.make_async_remote_copy(
                        src_ref=columns(queries, to).at[pl.ds(begin, count)],
                        dst_ref=qbuf.at[pl.ds(me * part + begin, count)],
                        send_sem=send_sem.at[2],
                        recv_sem=qsem.at[own_tile + ahead],
                        device_id=(span, to),
                        device_id_type=MESH,
                    ).start()

    def arrived(buf, sem, u):
        piece = block(buf, halo, u)
        pltpu.make_async_copy(piece, piece, sem.at[u]).wait()

    def forward(kind, buf, row, place):
        pltpu.make_async_remote_copy(
            src_ref=block(buf, halo, row * half + place),
            dst_ref=block(buf, (1 - row) * upper, place),
            send_sem=fwd_sem.at[kind],
            recv_sem=halo_sem.at[2 * kind + 1 - row],
            device_id=(row * above + (1 - row) * below, me),
            device_id_type=MESH,
        ).start()

    every(functools.partial(send, 0), True)
    every(functools.partial(send, 1), True)
    vbuf[pl.ds(upper + halo, units)] = jnp.zeros((units, UNIT, HD), jnp.bfloat16)

    def pass_on(kind, buf, sem):
        def step(row, place):
            arrived(buf, sem, row * half + place)
            forward(kind, buf, row, place)

        own[kind].wait()
        forward(kind, buf, side, depth * 2 + core)
        every(step, False)

    pass_on(0, kbuf, ksem)
    every(send_queries, True)
    pass_on(1, vbuf, vsem)

    for kind, buf in ((0, kbuf), (1, vbuf)):
        for end, first in ((0, 0), (1, upper)):
            region = buf.at[pl.ds(first, halo)]
            pltpu.make_async_copy(region, region, halo_sem.at[2 * kind + end]).wait()

    def tile_at(step):
        begin = lax.div(depth * 3 + 3, 4) - core
        turned = begin + (1 - 2 * core) * lax.div(step, 2)
        return lax.rem(side + step, 2) * PLANE + lax.rem(turned + PLANE, PLANE)

    def await_queries(step):
        tile = qbuf.at[pl.ds(tile_at(step) * units, units)]
        pltpu.make_async_copy(tile, tile, qsem.at[tile_at(step)]).wait()

    first_tile = span * own_tiles

    def whole(ref, first):
        return jnp.concatenate([ref[first + j] for j in range(units)], axis=0)

    def listed(tile, slot):
        entry = windows[slot, first_tile + tile]
        there = jnp.minimum(entry, 0) + 1
        near = jnp.clip(entry - first_tile + PLANE, 0, own_tiles + 2 * PLANE - 1)
        return there, there * near

    def key_tile(tile, slot):
        there, index = listed(tile, slot)
        return whole(kbuf, (index + (1 - there) * (tile + PLANE)) * units)

    def value_tile(tile, slot):
        there, index = listed(tile, slot)
        value = whole(vbuf, (index + (1 - there) * (own_tiles + 2 * PLANE)) * units)
        ones = jnp.full((TILE, HD), there.astype(jnp.float32)).astype(jnp.bfloat16)
        return jnp.concatenate([value, ones], axis=1)

    def load_queries(tile):
        return qbuf[pl.ds(tile * units, units)].reshape(TILE, HD)

    def score(tile, query, pack, highest):
        key = jnp.concatenate([key_tile(tile, pack * PACK + j) for j in range(PACK)], axis=0)
        fresh = lax.dot_general(
            query, key, (((1,), (1,)), ((), ())), preferred_element_type=jnp.float32
        )
        scores[pack] = fresh
        for at in range(0, PACK * TILE, HD):
            highest = jnp.maximum(highest, fresh[:, at : at + HD])
        return highest

    def mix(tile, shift, pack, total):
        value = jnp.concatenate([value_tile(tile, pack * PACK + j) for j in range(PACK)], axis=0)
        weights = jnp.exp2(scores[pack] * SCALE - shift).astype(jnp.bfloat16)
        part = jnp.dot(weights, value, preferred_element_type=jnp.float32)
        return part if total is None else total + part

    def lowest():
        return jnp.full((TILE, HD), -jnp.inf, jnp.float32)

    def shift_of(highest):
        return jnp.max(highest, axis=1, keepdims=True) * SCALE

    def finish(step, total):
        tile = tile_at(step)
        mixed = (total[:, :HD] / total[:, HD:]).astype(jnp.bfloat16)
        obuf[pl.ds(tile * units, units)] = mixed.reshape(units, UNIT, HD)

        gang = lax.div(tile, 3) * GANG
        for turn_of, pieces in enumerate(GIVES):
            @pl.when(lax.rem(tile, 3) == turn_of)
            def _():
                for place, begin, unit, count in pieces:
                    give(gang + place, begin, gang * part + unit, count)

    def give(u, begin, unit, count):
        mixed = obuf.at[pl.ds(unit, count)]
        home = columns(out, me).at[pl.ds(begin, count)]

        @pl.when(u == me)
        def _():
            pltpu.make_async_copy(mixed, home, orecv_sem).start()

        @pl.when(u != me)
        def _():
            pltpu.make_async_remote_copy(
                src_ref=mixed,
                dst_ref=home,
                send_sem=osend_sem,
                recv_sem=orecv_sem,
                device_id=(span, u),
                device_id_type=MESH,
            ).start()

    packs = NBR // PACK
    await_queries(0)
    query = load_queries(tile_at(0))
    highest = lowest()
    for pack in range(packs):
        highest = score(tile_at(0), query, pack, highest)

    def turn(step, shift):
        await_queries(step + 1)
        tile, later = tile_at(step), tile_at(step + 1)
        query = load_queries(later)
        highest, total = lowest(), None
        for pack in range(packs):
            total = mix(tile, shift, pack, total)
            highest = score(later, query, pack, highest)
        finish(step, total)
        return shift_of(highest)

    shift = lax.fori_loop(0, own_tiles - 1, turn, shift_of(highest))
    total = None
    for pack in range(packs):
        total = mix(tile_at(own_tiles - 1), shift, pack, total)
    finish(own_tiles - 1, total)

    sent = (wides - 1) * HD
    for kind, ref in enumerate((keys, values, queries)):
        region = ref.at[:, :, pl.ds(0, sent)]
        pltpu.make_async_copy(region, region, send_sem.at[kind]).wait()
    for kind, buf in ((0, kbuf), (1, vbuf)):
        region = buf.at[pl.ds(halo, own_units)]
        pltpu.make_async_copy(region, region, fwd_sem.at[kind]).wait()
    region = obuf.at[pl.ds(0, (wides - 1) * part)]
    pltpu.make_async_copy(region, region, osend_sem).wait()
    pltpu.make_async_copy(out, out, orecv_sem).wait()


def body(spans, wides, queries, keys, values, windows):
    rows, width = queries.shape
    part = rows // UNIT
    units = TILE // UNIT
    own_units = wides * part
    near = own_units + 2 * PLANE * units
    cut = [a.reshape(part, UNIT, width) for a in (queries, keys, values)]
    windows, *cut = [
        pltpu.with_memory_space_constraint(a, pltpu.HBM) for a in (windows.T, *cut)
    ]
    dma = pltpu.SemaphoreType.DMA
    out = pl.pallas_call(
        functools.partial(kernel, spans, wides),
        out_shape=jax.ShapeDtypeStruct((part, UNIT, width), jnp.bfloat16),
        in_specs=[pl.BlockSpec(memory_space=pltpu.SMEM)]
        + [pl.BlockSpec(memory_space=pltpu.HBM)] * 3,
        out_specs=pl.BlockSpec(memory_space=pl.ANY),
        scratch_shapes=[
            pltpu.VMEM((near, UNIT, HD), jnp.bfloat16),
            pltpu.VMEM((near + units, UNIT, HD), jnp.bfloat16),
            pltpu.VMEM((own_units, UNIT, HD), jnp.bfloat16),
            pltpu.VMEM((own_units, UNIT, HD), jnp.bfloat16),
            pltpu.VMEM((NBR // PACK, TILE, PACK * TILE), jnp.float32),
            dma((2,)),
            dma((wides,)),
            dma((wides,)),
            dma((own_units // units,)),
            dma((3,)),
            dma((4,)),
            dma((2,)),
            dma(()),
            dma(()),
        ],
        compiler_params=pltpu.CompilerParams(
            collective_id=0, has_side_effects=True, vmem_limit_bytes=48 << 20
        ),
        name="attend",
    )(windows, *cut)
    return out.reshape(rows, width)


def solution(mesh):
    return jax.shard_map(
        functools.partial(body, mesh.shape["span"], mesh.shape["wide"]),
        mesh=mesh,
        in_specs=(
            P(("span", "wide"), None),
            P(("span", "wide"), None),
            P(("span", "wide"), None),
            P(),
        ),
        out_specs=P(("span", "wide"), None),
        check_vma=False,
    )
```

```python
import functools
import math

import jax
import jax.numpy as jnp
from jax import lax
from jax.experimental import pallas as pl
from jax.experimental.pallas import tpu as pltpu
from jax.sharding import PartitionSpec as P

HD = 128
TILE = 384
PLANE = 6
NBR = 12
GANG = 8
UNIT = 48
PACK = 4
SPLITS = {2: ((0, 2, 0), (2, 1, 1)), 5: ((0, 1, 0), (1, 2, 1)), -1: ((0, 3, 0),)}
GIVES = (
    ((0, 0, 0, 3), (1, 0, 3, 3), (2, 0, 6, 2)),
    ((2, 2, 8, 1), (3, 0, 9, 3), (4, 0, 12, 3), (5, 0, 15, 1)),
    ((5, 1, 16, 2), (6, 0, 18, 3), (7, 0, 21, 3)),
)
MESH = pl.DeviceIdType.MESH
SCALE = HD**-0.5 * math.log2(math.e)


def kernel(
    spans, wides,
    windows, queries, keys, values, out,
    kbuf, vbuf, qbuf, obuf, scores,
    own_sem, ksem, vsem, qsem, send_sem, halo_sem, fwd_sem, osend_sem, orecv_sem,
):
    me = lax.axis_index("wide")
    span = lax.axis_index("span")
    above = lax.rem(span + 1, spans)
    below = lax.rem(span + spans - 1, spans)
    part = queries.shape[0]
    units = TILE // UNIT
    own_units = wides * part
    own_tiles = own_units // units
    halo = PLANE * units
    upper = halo + own_units
    half = wides // 2
    deep = half // 2
    side, depth, core = lax.div(me, half), lax.rem(lax.div(me, 2), deep), lax.rem(me, 2)

    def columns(ref, head):
        return ref.at[:, :, pl.ds(pl.multiple_of(head * HD, HD), HD)]

    def block(ref, first, index):
        return ref.at[pl.ds(first + index * part, part)]

    def peers(k, outward):
        up, down = depth + k, depth - k
        up = jnp.where(up >= deep, up - deep, up)
        down = jnp.where(down < 0, down + deep, down)
        found = []
        for j in range(4):
            there = core if j % 2 == 0 else 1 - core
            far = jnp.where(there == 1, up, down) if outward else jnp.where(core == 1, down, up)
            found.append((side if j < 2 else 1 - side, far * 2 + there))
        return found

    def far_first(step, outward):
        def ring(m, carry):
            k = deep // 2 + lax.div(m + 1, 2) * (1 - 2 * lax.rem(m, 2))
            for peer in peers(k, outward):
                step(*peer)
            return carry

        lax.fori_loop(0, deep - 1, ring, 0)
        for peer in peers(0, outward)[1:]:
            step(*peer)

    def every(step, outward):
        for peer in peers(0, outward)[1:]:
            step(*peer)

        def ring(k, carry):
            for peer in peers(k, outward):
                step(*peer)
            return carry

        lax.fori_loop(1, deep, ring, 0)

    own = [
        pltpu.make_async_copy(columns(keys, me), block(kbuf, halo, me), own_sem.at[0]),
        pltpu.make_async_copy(columns(values, me), block(vbuf, halo, me), own_sem.at[1]),
    ]
    for copy in own:
        copy.start()
    place_in_gang = lax.rem(me, GANG)
    own_tile = lax.div(me * part, units)
    whole_block = (place_in_gang != 2) & (place_in_gang != 5)
    for p in range(part):
        unit = me * part + p
        pltpu.make_async_copy(
            columns(queries, me).at[p], qbuf.at[unit], qsem.at[lax.div(unit, units)]
        ).start()

    barrier = pltpu.get_barrier_semaphore()

    def greet(row, place):
        to = row * half + place
        pl.semaphore_signal(barrier, inc=1, device_id=(span, to), device_id_type=MESH)

    for neighbour in (above, below):
        pl.semaphore_signal(barrier, inc=1, device_id=(neighbour, me), device_id_type=MESH)
    far_first(greet, True)
    pl.semaphore_wait(barrier, wides + 1)

    def send(kind, row, place):
        ref, buf, sem = ((keys, kbuf, ksem), (values, vbuf, vsem))[kind]
        to = row * half + place
        pltpu.make_async_remote_copy(
            src_ref=columns(ref, to),
            dst_ref=block(buf, halo, me),
            send_sem=send_sem.at[kind],
            recv_sem=sem.at[me],
            device_id=(span, to),
            device_id_type=MESH,
        ).start()

    def send_queries(row, place):
        to = row * half + place
        for member, pieces in SPLITS.items():
            mine = member == place_in_gang if member >= 0 else whole_block

            @pl.when(mine)
            def _():
                for begin, count, ahead in pieces:
                    pltpu.make_async_remote_copy(
                        src_ref=columns(queries, to).at[pl.ds(begin, count)],
                        dst_ref=qbuf.at[pl.ds(me * part + begin, count)],
                        send_sem=send_sem.at[2],
                        recv_sem=qsem.at[own_tile + ahead],
                        device_id=(span, to),
                        device_id_type=MESH,
                    ).start()

    def arrived(buf, sem, u):
        piece = block(buf, halo, u)
        pltpu.make_async_copy(piece, piece, sem.at[u]).wait()

    def forward(kind, buf, row, place):
        pltpu.make_async_remote_copy(
            src_ref=block(buf, halo, row * half + place),
            dst_ref=block(buf, (1 - row) * upper, place),
            send_sem=fwd_sem.at[kind],
            recv_sem=halo_sem.at[2 * kind + 1 - row],
            device_id=(row * above + (1 - row) * below, me),
            device_id_type=MESH,
        ).start()

    every(functools.partial(send, 0), True)
    every(functools.partial(send, 1), True)
    vbuf[pl.ds(upper + halo, units)] = jnp.zeros((units, UNIT, HD), jnp.bfloat16)

    def pass_on(kind, buf, sem):
        def step(row, place):
            arrived(buf, sem, row * half + place)
            forward(kind, buf, row, place)

        own[kind].wait()
        forward(kind, buf, side, depth * 2 + core)
        every(step, False)

    pass_on(0, kbuf, ksem)
    every(send_queries, True)
    pass_on(1, vbuf, vsem)

    for kind, buf in ((0, kbuf), (1, vbuf)):
        for end, first in ((0, 0), (1, upper)):
            region = buf.at[pl.ds(first, halo)]
            pltpu.make_async_copy(region, region, halo_sem.at[2 * kind + end]).wait()

    def tile_at(step):
        begin = lax.div(depth * 3 + 3, 4) - core
        turned = begin + (1 - 2 * core) * lax.div(step, 2)
        return lax.rem(side + step, 2) * PLANE + lax.rem(turned + PLANE, PLANE)

    def await_queries(step):
        tile = qbuf.at[pl.ds(tile_at(step) * units, units)]
        pltpu.make_async_copy(tile, tile, qsem.at[tile_at(step)]).wait()

    first_tile = span * own_tiles

    def whole(ref, first):
        return jnp.concatenate([ref[first + j] for j in range(units)], axis=0)

    def listed(tile, slot):
        entry = windows[slot, first_tile + tile]
        there = jnp.minimum(entry, 0) + 1
        near = jnp.clip(entry - first_tile + PLANE, 0, own_tiles + 2 * PLANE - 1)
        return there, there * near

    def key_tile(tile, slot):
        there, index = listed(tile, slot)
        return whole(kbuf, (index + (1 - there) * (tile + PLANE)) * units)

    def value_tile(tile, slot):
        there, index = listed(tile, slot)
        value = whole(vbuf, (index + (1 - there) * (own_tiles + 2 * PLANE)) * units)
        ones = jnp.full((TILE, HD), there.astype(jnp.float32)).astype(jnp.bfloat16)
        return jnp.concatenate([value, ones], axis=1)

    def load_queries(tile):
        return qbuf[pl.ds(tile * units, units)].reshape(TILE, HD)

    def score(tile, query, pack, highest):
        key = jnp.concatenate([key_tile(tile, pack * PACK + j) for j in range(PACK)], axis=0)
        fresh = lax.dot_general(
            query, key, (((1,), (1,)), ((), ())), preferred_element_type=jnp.float32
        )
        scores[pack] = fresh
        for at in range(0, PACK * TILE, HD):
            highest = jnp.maximum(highest, fresh[:, at : at + HD])
        return highest

    def mix(tile, shift, pack, total):
        value = jnp.concatenate([value_tile(tile, pack * PACK + j) for j in range(PACK)], axis=0)
        weights = jnp.exp2(scores[pack] * SCALE - shift).astype(jnp.bfloat16)
        part = jnp.dot(weights, value, preferred_element_type=jnp.float32)
        return part if total is None else total + part

    def lowest():
        return jnp.full((TILE, HD), -jnp.inf, jnp.float32)

    def shift_of(highest):
        return jnp.max(highest, axis=1, keepdims=True) * SCALE

    def finish(step, total):
        tile = tile_at(step)
        mixed = (total[:, :HD] / total[:, HD:]).astype(jnp.bfloat16)
        obuf[pl.ds(tile * units, units)] = mixed.reshape(units, UNIT, HD)

        gang = lax.div(tile, 3) * GANG
        for turn_of, pieces in enumerate(GIVES):
            @pl.when(lax.rem(tile, 3) == turn_of)
            def _():
                for place, begin, unit, count in pieces:
                    give(gang + place, begin, gang * part + unit, count)

    def give(u, begin, unit, count):
        mixed = obuf.at[pl.ds(unit, count)]
        home = columns(out, me).at[pl.ds(begin, count)]

        @pl.when(u == me)
        def _():
            pltpu.make_async_copy(mixed, home, orecv_sem).start()

        @pl.when(u != me)
        def _():
            pltpu.make_async_remote_copy(
                src_ref=mixed,
                dst_ref=home,
                send_sem=osend_sem,
                recv_sem=orecv_sem,
                device_id=(span, u),
                device_id_type=MESH,
            ).start()

    packs = NBR // PACK
    await_queries(0)
    query = load_queries(tile_at(0))
    highest = lowest()
    for pack in range(packs):
        highest = score(tile_at(0), query, pack, highest)

    def turn(step, shift):
        await_queries(step + 1)
        tile, later = tile_at(step), tile_at(step + 1)
        query = load_queries(later)
        highest, total = lowest(), None
        for pack in range(packs):
            total = mix(tile, shift, pack, total)
            highest = score(later, query, pack, highest)
        finish(step, total)
        return shift_of(highest)

    shift = lax.fori_loop(0, own_tiles - 1, turn, shift_of(highest))
    total = None
    for pack in range(packs):
        total = mix(tile_at(own_tiles - 1), shift, pack, total)
    finish(own_tiles - 1, total)

    sent = (wides - 1) * HD
    for kind, ref in enumerate((keys, values, queries)):
        region = ref.at[:, :, pl.ds(0, sent)]
        pltpu.make_async_copy(region, region, send_sem.at[kind]).wait()
    for kind, buf in ((0, kbuf), (1, vbuf)):
        region = buf.at[pl.ds(halo, own_units)]
        pltpu.make_async_copy(region, region, fwd_sem.at[kind]).wait()
    region = obuf.at[pl.ds(0, (wides - 1) * part)]
    pltpu.make_async_copy(region, region, osend_sem).wait()
    pltpu.make_async_copy(out, out, orecv_sem).wait()


def body(spans, wides, queries, keys, values, windows):
    rows, width = queries.shape
    part = rows // UNIT
    units = TILE // UNIT
    own_units = wides * part
    near = own_units + 2 * PLANE * units
    cut = [a.reshape(part, UNIT, width) for a in (queries, keys, values)]
    windows, *cut = [
        pltpu.with_memory_space_constraint(a, pltpu.HBM) for a in (windows.T, *cut)
    ]
    dma = pltpu.SemaphoreType.DMA
    out = pl.pallas_call(
        functools.partial(kernel, spans, wides),
        out_shape=jax.ShapeDtypeStruct((part, UNIT, width), jnp.bfloat16),
        in_specs=[pl.BlockSpec(memory_space=pltpu.SMEM)]
        + [pl.BlockSpec(memory_space=pltpu.HBM)] * 3,
        out_specs=pl.BlockSpec(memory_space=pl.ANY),
        scratch_shapes=[
            pltpu.VMEM((near, UNIT, HD), jnp.bfloat16),
            pltpu.VMEM((near + units, UNIT, HD), jnp.bfloat16),
            pltpu.VMEM((own_units, UNIT, HD), jnp.bfloat16),
            pltpu.VMEM((own_units, UNIT, HD), jnp.bfloat16),
            pltpu.VMEM((NBR // PACK, TILE, PACK * TILE), jnp.float32),
            dma((2,)),
            dma((wides,)),
            dma((wides,)),
            dma((own_units // units,)),
            dma((3,)),
            dma((4,)),
            dma((2,)),
            dma(()),
            dma(()),
        ],
        compiler_params=pltpu.CompilerParams(
            collective_id=0, has_side_effects=True, vmem_limit_bytes=48 << 20
        ),
        name="attend",
    )(windows, *cut)
    return out.reshape(rows, width)


def solution(mesh):
    return jax.shard_map(
        functools.partial(body, mesh.shape["span"], mesh.shape["wide"]),
        mesh=mesh,
        in_specs=(
            P(("span", "wide"), None),
            P(("span", "wide"), None),
            P(("span", "wide"), None),
            P(),
        ),
        out_specs=P(("span", "wide"), None),
        check_vma=False,
    )
```
